32 devices in a mesh: dp: 8 (over z, core), ctx: 4 (over y, x).
Axes of the slice: x: 2, y: 2, z: 4, core: 2. Of those that a mesh axis runs over, the one named last changes fastest.
Arguments:
- query: bfloat16 [8, 512, 1024], P('dp', 'ctx'), may hold values from -5 to 5
- key: bfloat16 [8, 512, 512], P('dp', 'ctx'), may hold values from -5 to 5
- value: bfloat16 [8, 512, 512], P('dp', 'ctx'), may hold values from -12 to 12
- out_weight: bfloat16 [1024, 2304], P('dp')
- post_gain: float32 [2304], replicated, may hold values from 0.25 to 4
- grad_out: bfloat16 [8, 512, 2304], P('dp', 'ctx'), may hold values from -6 to 6
- block_lists: int32 [8, 4, 3], P('dp', 'ctx'), may hold values from -1 to 2, as said below
Outputs:
- grad_query: bfloat16 [8, 512, 1024], P('dp', 'ctx')
- grad_key: bfloat16 [8, 512, 512], P('dp', 'ctx')
- grad_value: bfloat16 [8, 512, 512], P('dp', 'ctx')
- grad_wo: float32 [1024, 2304], P('dp')
- grad_gain: float32 [2304], replicated
The draws below stay inside these ranges and needn't reach their ends.
Inputs may be any that keep to these rules, and one draw needn't show every extreme that they name: `block_lists`: row b of each sequence holds, in its first min(3, b) slots, different block numbers below b, one of which is b - 1 when b >= 1, and -1 in its other slots.
All inputs are finite; a program needn't handle non-finite values.
Results may differ from the reference program's by a relative error of at most 0.02.
Values may be sent and summed in bfloat16 or wider, within the bound.
A program may use at most 64 MiB of HBM per device.

```python
import math
import jax
import jax.numpy as jnp
from jax import lax

D = 2304
HD = 256
HQ = 4
HK = 2
BLK = 128
TOPK = 3
LEN = 512
NBLK = 4
SEQS = 8


def drawn_pair(key):
    query_key = jax.random.fold_in(key, 101)
    key_key = jax.random.fold_in(key, 102)
    query_base = jnp.clip(jax.random.normal(query_key, (SEQS, LEN, HQ * HD), jnp.float32), -4.0, 4.0)
    key_base = jnp.clip(jax.random.normal(key_key, (SEQS, LEN, HK * HD), jnp.float32), -4.0, 4.0)
    return (query_base, key_base)


def draw_query(key, part):
    return drawn_pair(key)[0].astype(jnp.bfloat16)


def draw_key(key, part):
    return drawn_pair(key)[1].astype(jnp.bfloat16)


def draw_value(key, part):
    base_key = jax.random.fold_in(key, 201)
    scale_key = jax.random.fold_in(key, 202)
    base = jnp.clip(jax.random.normal(base_key, (SEQS, LEN, HK * HD), jnp.float32), -4.0, 4.0)
    row_scale = jnp.exp(jax.random.uniform(scale_key, (SEQS, LEN, 1), jnp.float32, -1.2, 1.0986))
    return (base * row_scale).astype(jnp.bfloat16)


def draw_out_weight(key, part):
    base_key = jax.random.fold_in(key, 301)
    scale_key = jax.random.fold_in(key, 302)
    fan_factor = float(HQ * HD) ** (-0.5)
    base = jnp.clip(jax.random.normal(base_key, (HQ * HD, D), jnp.float32), -4.0, 4.0)
    column_scale = jnp.exp(jax.random.uniform(scale_key, (1, D), jnp.float32, -1.2, 1.0986))
    return (base * column_scale * fan_factor).astype(jnp.bfloat16)


def draw_block_lists(key, part):
    scores = jax.random.randint(jax.random.fold_in(key, 401), (SEQS, NBLK, NBLK), 0, 1048576)
    columns = jnp.arange(NBLK, dtype=jnp.int32)
    distinct = scores * NBLK + columns[None, None, :]
    previous = columns[None, :] == columns[:, None] - 1
    distinct = jnp.where(previous[None, :, :], 1048576 * NBLK + NBLK, distinct)
    earlier = columns[None, :] < columns[:, None]
    ranked = jnp.where(earlier[None, :, :], distinct, -1)
    best, picked = lax.top_k(ranked, TOPK)
    return jnp.where(best >= 0, picked, -1).astype(jnp.int32)


def levels(stream_key, dims, split, least, top_value):
    loudness, own = 1.0, jax.random.fold_in(stream_key, 6)
    for axis_at, blocks in split:
        draws = jnp.exp(jax.random.uniform(jax.random.fold_in(own, axis_at), (blocks,), jnp.float32, least / len(split), top_value / len(split)))
        loudness = loudness * jnp.repeat(draws, dims[axis_at] // blocks).reshape([-1 if axis == axis_at else 1 for axis in range(len(dims))])
    return loudness


def gaussian(rng, dims, spread, limit, shards=(), held_as=jnp.bfloat16):
    entries = spread * jax.random.normal(rng, dims, jnp.float32)
    if shards:
        entries = entries * levels(rng, dims, shards, -0.22, 0.18)
    return jnp.clip(entries, -limit, limit).astype(held_as)


def setup_inputs(seed: int = 0) -> dict:
    key_list = jax.random.split(jax.random.key(seed), 8)
    return {
        "query": draw_query(jax.random.fold_in(key_list[7], 71), 0),
        "key": draw_key(jax.random.fold_in(key_list[7], 71), 0),
        "value": draw_value(jax.random.fold_in(key_list[7], 71), 0),
        "out_weight": draw_out_weight(jax.random.fold_in(key_list[7], 71), 0),
        "post_gain": jnp.clip(jnp.exp(jax.random.uniform(key_list[4], (D,), jnp.float32, math.log(0.25), math.log(4.0))), 0.25, 4.0),
        "grad_out": gaussian(key_list[5], (SEQS, LEN, D), 1.0, 6.0, ((0, 8), (1, 4))),
        "block_lists": draw_block_lists(jax.random.fold_in(key_list[7], 71), 0),
    }


SCALE = 0.0625
NEGATIVE = -1e+30
EPSILON = 1e-06

def to_low(values_in):
    return lax.optimization_barrier(values_in.astype(jnp.bfloat16))

def one_sequence(query_seq, key_seq, value_seq, grad_seq, block_ids, out_weight, post_gain):
    groups = HQ // HK
    positions = jnp.arange(LEN, dtype=jnp.int32)
    blocks = positions // BLK
    numbers = jnp.arange(NBLK, dtype=jnp.int32)
    chosen = jnp.any(block_ids[:, :, None] == numbers[None, None, :], axis=1)
    chosen = jnp.broadcast_to(chosen[:, None, :, None], (NBLK, BLK, NBLK, BLK)).reshape(LEN, LEN)
    own_block = (blocks[:, None] == blocks[None, :]) & (positions[None, :] <= positions[:, None])
    allowed = chosen | own_block
    queries = query_seq.astype(jnp.float32).reshape(LEN, HK, groups, HD)
    key_heads = key_seq.astype(jnp.float32).reshape(LEN, HK, HD)
    value_heads = value_seq.astype(jnp.float32).reshape(LEN, HK, HD)
    logits = jnp.einsum('tkgd,skd->kgts', queries, key_heads) * SCALE
    logits = jnp.where(allowed, logits, NEGATIVE)
    row_max = lax.optimization_barrier(jnp.max(logits, axis=-1))
    exp_total = lax.optimization_barrier(jnp.sum(jnp.where(allowed, jnp.exp(logits - row_max[..., None]), 0.0), axis=-1))
    log_total = row_max + jnp.log(exp_total)
    attn_probs = jnp.where(allowed, jnp.exp(logits - log_total[..., None]), 0.0)
    probs_low = to_low(attn_probs).astype(jnp.float32)
    heads_out = to_low(jnp.einsum('kgts,skd->tkgd', probs_low, value_heads)).reshape(LEN, HQ * HD)
    mixed_out = jnp.dot(heads_out, out_weight, preferred_element_type=jnp.float32)
    inv_rms = lax.rsqrt(lax.optimization_barrier(jnp.mean(mixed_out * mixed_out, axis=-1, keepdims=True)) + EPSILON)
    upstream = grad_seq.astype(jnp.float32)
    scaled = upstream * post_gain
    gain_term = lax.optimization_barrier(jnp.sum(upstream * mixed_out * inv_rms, axis=0))
    grad_mixed = to_low(inv_rms * (scaled - mixed_out * inv_rms * inv_rms * lax.optimization_barrier(jnp.mean(scaled * mixed_out, axis=-1, keepdims=True))))
    wo_term = jnp.dot(heads_out.T, grad_mixed, preferred_element_type=jnp.float32)
    grad_heads = to_low(jnp.dot(grad_mixed, out_weight.T, preferred_element_type=jnp.float32))
    grad_float = grad_heads.astype(jnp.float32).reshape(LEN, HK, groups, HD)
    heads_float = heads_out.astype(jnp.float32).reshape(LEN, HK, groups, HD)
    delta = jnp.einsum('tkgd,tkgd->kgt', grad_float, heads_float)
    grad_probs = jnp.einsum('tkgd,skd->kgts', grad_float, value_heads)
    grad_logits = to_low(jnp.where(allowed, attn_probs * (grad_probs - delta[..., None]) * SCALE, 0.0)).astype(jnp.float32)
    grad_query = jnp.einsum('kgts,skd->tkgd', grad_logits, key_heads).astype(jnp.bfloat16).reshape(LEN, HQ * HD)
    grad_key = jnp.einsum('kgts,tkgd->skd', grad_logits, queries).astype(jnp.bfloat16).reshape(LEN, HK * HD)
    grad_value = jnp.einsum('kgts,tkgd->skd', probs_low, grad_float).astype(jnp.bfloat16).reshape(LEN, HK * HD)
    return (grad_query, grad_key, grad_value, wo_term, gain_term)

def reference(query, key, value, out_weight, post_gain, grad_out, block_lists):

    def per_sequence(carried, inputs):
        wo_total, gain_total = carried
        query_seq, key_seq, value_seq, grad_seq, block_ids = inputs
        results = one_sequence(query_seq, key_seq, value_seq, grad_seq, block_ids, out_weight, post_gain)
        return ((wo_total + results[3], gain_total + results[4]), (results[0], results[1], results[2]))
    start_state = (jnp.zeros((HQ * HD, D), jnp.float32), jnp.zeros((D,), jnp.float32))
    sums, grads = lax.scan(per_sequence, start_state, (query, key, value, grad_out, block_lists))
    return (grads[0], grads[1], grads[2], sums[0] / SEQS, sums[1] / SEQS)
```

```python
import functools
import jax
import jax.numpy as jnp
from jax import lax
from jax.experimental import pallas as pl
from jax.experimental.pallas import tpu as pltpu
from jax.sharding import PartitionSpec as P

HD = 256
HQ = 4
HK = 2
BLK = 128
TOPK = 3
LANE = 128
SCALE = 0.0625
NEGATIVE = -1e30
EPSILON = 1e-06
MESH = pl.DeviceIdType.MESH
F32 = jnp.float32
BF16 = jnp.bfloat16


def dot(a, b, dims):
    return lax.dot_general(a, b, (dims, ((), ())), preferred_element_type=F32)


NN = ((1,), (0,))
NT = ((1,), (1,))
TN = ((0,), (0,))


def kernel(
    n, ndp, q, k, v, w, gain, go, bl,
    dq_o, dk_o, dv_o, wo_o, gain_o,
    kbuf, vbuf, wc, goc, hall, probs, mixed, gm, stat, ghs, ghr, gho, gwf, gws, gwr, zs, zr,
    dkf, dvf, dks, dvs, dkr, dvr, wog, gp, gpr, gz, gg,
    kv_s, kv_r, w_s, w_r, wp_s, wp_r, go_s, go_r, h_s, h_r, st_s, st_r, gh_s, gh_r,
    gw_s, gw_r, z_s, z_r, d_s, d_r, wo_s, wo_r, gn_s, gn_r,
):
    d = lax.axis_index("dp")
    me = lax.axis_index("ctx")
    core = lax.rem(d, 2)
    z = d // 2
    nz = ndp // 2
    partner = d + 1 - 2 * core
    width = gain.shape[1]
    tiles = width // LANE
    wt = -(-tiles // n)
    win = wt * LANE
    rows = w.shape[0]
    keys = n * BLK
    seqs = float(ndp)

    def start_of(c):
        if isinstance(c, int):
            return min(tiles * c // n, tiles - wt)
        return jnp.minimum(tiles * c // n, tiles - wt)

    def window(c):
        return pl.ds(pl.multiple_of(start_of(c) * LANE, LANE), win)

    def blk(b):
        return pl.ds(pl.multiple_of(b * BLK, BLK), BLK)

    def wrows(b):
        return pl.ds(pl.multiple_of(b * rows, rows), rows)

    def ahead(i):
        return lax.rem(me + i, n)

    def behind(i):
        return lax.rem(me + n - i, n)

    def zpeer(i):
        return lax.rem(z + i, nz) * 2 + core

    def zbehind(i):
        return lax.rem(z + nz - i, nz)

    def copy(src, dst, ss, rs, dev):
        return pltpu.make_async_remote_copy(
            src_ref=src, dst_ref=dst, send_sem=ss, recv_sem=rs, device_id=dev, device_id_type=MESH
        )

    barrier = pltpu.get_barrier_semaphore()
    for i in range(1, n):
        pl.semaphore_signal(barrier, inc=1, device_id=(d, ahead(i)), device_id_type=MESH)
    for i in range(1, nz):
        pl.semaphore_signal(barrier, inc=1, device_id=(zpeer(i), me), device_id_type=MESH)
    pl.semaphore_signal(barrier, inc=1, device_id=(partner, me), device_id_type=MESH)
    pl.semaphore_wait(barrier, n + nz - 1)

    def kv_copies(i, block, dev):
        return [
            copy(k, kbuf.at[blk(block), :], kv_s.at[0, i], kv_r.at[0, i], (d, dev)),
            copy(v, vbuf.at[blk(block), :], kv_s.at[1, i], kv_r.at[1, i], (d, dev)),
        ]

    for i in range(1, n):
        @pl.when(me + i < n)
        def _(i=i):
            for c in kv_copies(i, me, ahead(i)):
                c.start()

    def w_copy(i):
        return copy(w.at[:, window(me)], wc.at[wrows(d), :], w_s.at[i], w_r.at[i], (zpeer(i), me))

    def w_arrived(i):
        there = wc.at[wrows(zbehind(i) * 2 + core), :]
        return copy(there, there, w_s.at[i], w_r.at[i], (zpeer(i), me))

    def w_relay(i):
        there = wc.at[wrows(zbehind(i) * 2 + core), :]
        src = w.at[:, window(me)] if i == 0 else there
        return copy(src, there, wp_s.at[i], wp_r.at[i], (partner, me))

    def w_relayed(i):
        there = wc.at[wrows(zbehind(i) * 2 + 1 - core), :]
        return copy(there, there, wp_s.at[i], wp_r.at[i], (partner, me))

    for i in range(1, nz):
        w_copy(i).start()
    w_relay(0).start()
    wc[wrows(d), :] = w[:, window(me)]
    kbuf[blk(me), :] = k[...]
    vbuf[blk(me), :] = v[...]
    goc[blk(me), :] = go[:, window(me)]
    for u in range(1, n):
        @pl.when(u > me)
        def _(u=u):
            kbuf[u * BLK : (u + 1) * BLK, :] = jnp.zeros((BLK, kbuf.shape[1]), BF16)
            vbuf[u * BLK : (u + 1) * BLK, :] = jnp.zeros((BLK, vbuf.shape[1]), BF16)

    for i in range(1, n):
        @pl.when(me >= i)
        def _(i=i):
            for c in kv_copies(i, behind(i), ahead(i)):
                c.wait_recv()

    def go_copy(i, block):
        return copy(
            go.at[:, window(ahead(i))], goc.at[blk(block), :], go_s.at[i], go_r.at[i], (d, ahead(i))
        )

    for i in range(1, n):
        go_copy(i, me).start()

    qpos = lax.rem(lax.broadcasted_iota(jnp.int32, (2 * BLK, keys), 0), BLK)
    kpos = lax.broadcasted_iota(jnp.int32, (2 * BLK, keys), 1)
    allowed = (kpos <= qpos + me * BLK) & (kpos >= me * BLK)
    for s in range(TOPK):
        first = bl[0, s] * BLK
        allowed = allowed | ((kpos >= first) & (kpos < first + BLK) & (kpos >= 0))

    def pair(x, j):
        return jnp.concatenate(
            [x[:, 2 * j * HD : (2 * j + 1) * HD], x[:, (2 * j + 1) * HD : (2 * j + 2) * HD]], axis=0
        )

    def h_copy(j, i, block):
        ref = hall.at[blk(block), pl.ds(j * 2 * HD, 2 * HD)]
        return copy(ref, ref, h_s.at[j, i], h_r.at[j, i], (d, ahead(i)))

    for j in range(HK):
        logits = dot(pair(q, j), kbuf[:, j * HD : (j + 1) * HD], NT) * SCALE
        logits = jnp.where(allowed, logits, NEGATIVE)
        e = jnp.exp(logits - jnp.max(logits, axis=-1, keepdims=True))
        p = e / jnp.sum(e, axis=-1, keepdims=True)
        probs[j] = p
        out = dot(p.astype(BF16), vbuf[:, j * HD : (j + 1) * HD], NN).astype(BF16)
        hall[blk(me), 2 * j * HD : (2 * j + 1) * HD] = out[:BLK]
        hall[blk(me), (2 * j + 1) * HD : (2 * j + 2) * HD] = out[BLK:]
        for i in range(1, n):
            h_copy(j, i, me).start()

    for i in range(1, nz):
        w_arrived(i).wait_recv()
        w_relay(i).start()
    for i in range(nz):
        w_relayed(i).wait_recv()

    col = lax.broadcasted_iota(jnp.int32, (1, win), 1) // LANE + start_of(me)
    live = (col >= tiles * me // n) & (col < tiles * (me + 1) // n)
    gain_win = gain[:, window(me)]
    lane = lax.broadcasted_iota(jnp.int32, (BLK, LANE), 1)
    for i in range(n):
        b = behind(i)
        if i:
            for j in range(HK):
                h_copy(j, i, b).wait_recv()
            go_copy(i, b).wait_recv()
        part = jnp.where(live, dot(hall[blk(b), :], wc[...], NN), 0.0)
        mixed[blk(b), :] = part
        scaled = goc[blk(b), :].astype(F32) * gain_win
        square = jnp.sum(part * part, axis=-1, keepdims=True)
        cross = jnp.sum(scaled * part, axis=-1, keepdims=True)
        both = jnp.where(lane == 0, square, jnp.where(lane == 1, cross, 0.0))
        stat[me, b] = jnp.transpose(both)[:8]

    def st_copy(i, slot):
        return copy(stat.at[slot], stat.at[slot], st_s.at[i], st_r.at[i], (d, ahead(i)))

    for i in range(1, n):
        st_copy(i, me).start()
    for i in range(1, n):
        st_copy(i, behind(i)).wait_recv()

    def gh_copy(i):
        return copy(ghs.at[i], ghr.at[i], gh_s.at[i], gh_r.at[i], (d, ahead(i)))

    gain_part = jnp.zeros((1, win), F32)
    for step in range(n):
        i = (step + 1) % n
        b = ahead(i)
        total = stat[0, b]
        for c in range(1, n):
            total = total + stat[c, b]
        turned = jnp.transpose(jnp.concatenate([total] * (LANE // 8), axis=0))
        inv = lax.rsqrt(turned[:, 0:1] / width + EPSILON)
        cross = turned[:, 1:2] / width
        part = mixed[blk(b), :]
        upstream = goc[blk(b), :].astype(F32)
        grad = inv * (upstream * gain_win - part * (inv * inv * cross))
        grad = jnp.where(live, grad, 0.0).astype(BF16)
        gm[blk(b), :] = grad
        back = dot(grad, wc[...], NT)
        if i:
            ghs[i] = back.astype(BF16)
            gh_copy(i).start()
        else:
            gho[...] = back
        gain_part = gain_part + jnp.sum(upstream * part * inv, axis=0, keepdims=True)
    gp[...] = jnp.broadcast_to(gain_part, (8, win))

    def gp_copy():
        return copy(gp, gpr, gn_s.at[0], gn_r.at[0], (partner, me))

    gp_copy().start()

    for j in range(HQ):
        both = dot(hall[:, j * HD : (j + 1) * HD], gm[...], TN)
        gwf[j * HD : (j + 1) * HD, :] = both
        gws[j * HD : (j + 1) * HD, :] = both.astype(BF16)

    def gw_copy(zz):
        return copy(
            gws.at[wrows(zz * 2 + 1 - core), :], gwr.at[zz], gw_s.at[zz], gw_r.at[zz], (partner, me)
        )

    def z_copy(i):
        return copy(zs.at[i], zr.at[i], z_s.at[i], z_r.at[i], (zpeer(i), me))

    def gz_copy(i, slot):
        return copy(gz.at[slot], gz.at[slot], gn_s.at[i], gn_r.at[i], (zpeer(i), me))

    for zz in range(nz):
        gw_copy(zz).start()
    gp_copy().wait_recv()
    gz[z] = gp[...] + gpr[...]
    for zz in range(nz):
        gw_copy(zz).wait_recv()
    for i in range(1, nz):
        zz = lax.rem(z + i, nz)
        zs[i] = (gwf[wrows(zz * 2 + core), :] + gwr[zz].astype(F32)).astype(BF16)
        z_copy(i).start()
        gz_copy(i, z).start()

    back = gho[...]
    for i in range(1, n):
        gh_copy(i).wait_recv()
        back = back + ghr[i].astype(F32)
    back = back.astype(BF16)
    held = hall[blk(me), :]
    for j in range(HK):
        gj = pair(back, j)
        oj = pair(held, j)
        delta = jnp.sum(gj.astype(F32) * oj.astype(F32), axis=-1, keepdims=True)
        span = slice(j * HD, (j + 1) * HD)
        gprob = dot(gj, vbuf[:, span], NT)
        p = probs[j]
        ds = (p * (gprob - delta) * SCALE).astype(BF16)
        dv = dot(p.astype(BF16), gj, TN)
        dk = dot(ds, pair(q, j), TN)
        dvf[:, span] = dv
        dkf[:, span] = dk
        dvs[:, span] = dv.astype(BF16)
        dks[:, span] = dk.astype(BF16)
        dq = dot(ds, kbuf[:, span], NN).astype(BF16)
        dq_o[:, 2 * j * HD : (2 * j + 1) * HD] = dq[:BLK]
        dq_o[:, (2 * j + 1) * HD : (2 * j + 2) * HD] = dq[BLK:]

    def d_copies(i):
        dev = (d, behind(i))
        return [
            copy(dks.at[blk(behind(i)), :], dkr.at[i], d_s.at[0, i], d_r.at[0, i], dev),
            copy(dvs.at[blk(behind(i)), :], dvr.at[i], d_s.at[1, i], d_r.at[1, i], dev),
        ]

    for i in range(1, n):
        @pl.when(me >= i)
        def _(i=i):
            for c in d_copies(i):
                c.start()

    total = gwf[wrows(d), :] + gwr[z].astype(F32)
    for i in range(1, nz):
        z_copy(i).wait_recv()
        total = total + zr[i].astype(F32)
        gz_copy(i, zbehind(i)).wait_recv()
    wog[me] = total.astype(BF16)
    small = gz[0]
    for zz in range(1, nz):
        small = small + gz[zz]
    gg[me] = small

    def wo_copies(i, slot):
        dev = (d, ahead(i))
        return [
            copy(wog.at[slot], wog.at[slot], wo_s.at[0, i], wo_r.at[0, i], dev),
            copy(gg.at[slot], gg.at[slot], wo_s.at[1, i], wo_r.at[1, i], dev),
        ]

    for i in range(1, n):
        for c in wo_copies(i, me):
            c.start()

    dkf[blk(0), :] = dkf[blk(me), :]
    dvf[blk(0), :] = dvf[blk(me), :]
    for i in range(1, n):
        @pl.when(me + i < n)
        def _(i=i):
            for c in d_copies(i):
                c.wait_recv()
            dkf[blk(0), :] += dkr[i].astype(F32)
            dvf[blk(0), :] += dvr[i].astype(F32)

    dk_o[...] = dkf[blk(0), :].astype(BF16)
    dv_o[...] = dvf[blk(0), :].astype(BF16)

    for i in range(1, n):
        for c in wo_copies(i, behind(i)):
            c.wait_recv()
    for c in range(n):
        lo, hi = tiles * c // n, tiles * (c + 1) // n
        at = (lo - start_of(c)) * LANE
        span = slice(lo * LANE, hi * LANE)
        wo_o[:, span] = wog[c, :, at : at + (hi - lo) * LANE]
        gain_o[:, span] = gg[c, 0:1, at : at + (hi - lo) * LANE] / seqs

    for i in range(1, n):
        @pl.when(me + i < n)
        def _(i=i):
            for c in kv_copies(i, me, ahead(i)):
                c.wait_send()

        @pl.when(me >= i)
        def _(i=i):
            for c in d_copies(i):
                c.wait_send()

        go_copy(i, me).wait_send()
        for j in range(HK):
            h_copy(j, i, me).wait_send()
        st_copy(i, me).wait_send()
        gh_copy(i).wait_send()
        for c in wo_copies(i, me):
            c.wait_send()
    for i in range(1, nz):
        w_copy(i).wait_send()
        z_copy(i).wait_send()
        gz_copy(i, z).wait_send()
    for i in range(nz):
        w_relay(i).wait_send()
        gw_copy(i).wait_send()
    gp_copy().wait_send()


def per_device(n, ndp, query, key, value, out_weight, post_gain, grad_out, block_lists):
    width = out_weight.shape[1]
    rows = out_weight.shape[0]
    tiles = width // LANE
    win = -(-tiles // n) * LANE
    keys = n * BLK
    nz = ndp // 2
    qw, kw = HQ * HD, HK * HD
    vm = pl.BlockSpec(memory_space=pltpu.VMEM)
    dma = pltpu.SemaphoreType.DMA
    dq, dk, dv, wo, gain = pl.pallas_call(
        functools.partial(kernel, n, ndp),
        out_shape=(
            jax.ShapeDtypeStruct((BLK, qw), BF16),
            jax.ShapeDtypeStruct((BLK, kw), BF16),
            jax.ShapeDtypeStruct((BLK, kw), BF16),
            jax.ShapeDtypeStruct((rows, width), BF16),
            jax.ShapeDtypeStruct((1, width), F32),
        ),
        in_specs=[vm] * 6 + [pl.BlockSpec(memory_space=pltpu.SMEM)],
        out_specs=[vm] * 5,
        scratch_shapes=[
            pltpu.VMEM((keys, kw), BF16),
            pltpu.VMEM((keys, kw), BF16),
            pltpu.VMEM((qw, win), BF16),
            pltpu.VMEM((keys, win), BF16),
            pltpu.VMEM((keys, qw), BF16),
            pltpu.VMEM((HK, 2 * BLK, keys), F32),
            pltpu.VMEM((keys, win), F32),
            pltpu.VMEM((keys, win), BF16),
            pltpu.VMEM((n, n, 8, LANE), F32),
            pltpu.VMEM((n, BLK, qw), BF16),
            pltpu.VMEM((n, BLK, qw), BF16),
            pltpu.VMEM((BLK, qw), F32),
            pltpu.VMEM((qw, win), F32),
            pltpu.VMEM((qw, win), BF16),
            pltpu.VMEM((nz, rows, win), BF16),
            pltpu.VMEM((nz, rows, win), BF16),
            pltpu.VMEM((nz, rows, win), BF16),
            pltpu.VMEM((keys, kw), F32),
            pltpu.VMEM((keys, kw), F32),
            pltpu.VMEM((keys, kw), BF16),
            pltpu.VMEM((keys, kw), BF16),
            pltpu.VMEM((n, BLK, kw), BF16),
            pltpu.VMEM((n, BLK, kw), BF16),
            pltpu.VMEM((n, rows, win), BF16),
            pltpu.VMEM((8, win), F32),
            pltpu.VMEM((8, win), F32),
            pltpu.VMEM((nz, 8, win), F32),
            pltpu.VMEM((n, 8, win), F32),
            dma((2, n)), dma((2, n)), dma((nz,)), dma((nz,)), dma((nz,)), dma((nz,)),
            dma((n,)), dma((n,)), dma((HK, n)), dma((HK, n)), dma((n,)), dma((n,)),
            dma((n,)), dma((n,)), dma((nz,)), dma((nz,)), dma((nz,)), dma((nz,)),
            dma((2, n)), dma((2, n)), dma((2, n)), dma((2, n)), dma((nz,)), dma((nz,)),
        ],
        compiler_params=pltpu.CompilerParams(
            collective_id=0, has_side_effects=True, vmem_limit_bytes=56 * 2**20
        ),
        cost_estimate=pl.CostEstimate(flops=4 * 10**9, bytes_accessed=6 * 10**6, transcendentals=262144),
    )(
        query[0], key[0], value[0], out_weight, post_gain.reshape(1, width), grad_out[0], block_lists[0],
    )
    return (dq[None], dk[None], dv[None], wo.astype(F32) / ndp, gain.reshape(width))


def solution(mesh):
    n, ndp = mesh.shape["ctx"], mesh.shape["dp"]
    seq = P("dp", "ctx", None)
    return jax.shard_map(
        functools.partial(per_device, n, ndp),
        mesh=mesh,
        in_specs=(seq, seq, seq, P("dp", None), P(), seq, seq),
        out_specs=(seq, seq, seq, P("dp", None), P()),
        check_vma=False,
    )
```

```python
import functools
import jax
import jax.numpy as jnp
from jax import lax
from jax.experimental import pallas as pl
from jax.experimental.pallas import tpu as pltpu
from jax.sharding import PartitionSpec as P

HD = 256
HQ = 4
HK = 2
BLK = 128
TOPK = 3
LANE = 128
SCALE = 0.0625
NEGATIVE = -1e30
EPSILON = 1e-06
MESH = pl.DeviceIdType.MESH
F32 = jnp.float32
BF16 = jnp.bfloat16


def dot(a, b, dims):
    return lax.dot_general(a, b, (dims, ((), ())), preferred_element_type=F32)


NN = ((1,), (0,))
NT = ((1,), (1,))
TN = ((0,), (0,))


def kernel(
    n, ndp, q, k, v, w, gain, go, bl,
    dq_o, dk_o, dv_o, wo_o, gain_o,
    kbuf, vbuf, wc, goc, hall, probs, mixed, gm, stat, ghs, ghr, gho, gwf, gws, gwr, zs, zr,
    dkf, dvf, dks, dvs, dkr, dvr, wog, gp, gpr, gz, gg,
    kv_s, kv_r, w_s, w_r, wp_s, wp_r, go_s, go_r, h_s, h_r, st_s, st_r, gh_s, gh_r,
    gw_s, gw_r, z_s, z_r, d_s, d_r, wo_s, wo_r, gn_s, gn_r, gg_s, gg_r,
):
    d = lax.axis_index("dp")
    me = lax.axis_index("ctx")
    core = lax.rem(d, 2)
    z = d // 2
    nz = ndp // 2
    partner = d + 1 - 2 * core
    width = w.shape[1]
    square = n == 4
    tiles = width // LANE
    wt = -(-tiles // n)
    win = wt * LANE
    rows = w.shape[0]
    keys = n * BLK
    seqs = float(ndp)

    def start_of(c):
        if isinstance(c, int):
            return min(tiles * c // n, tiles - wt)
        return jnp.minimum(tiles * c // n, tiles - wt)

    def window(c):
        return pl.ds(pl.multiple_of(start_of(c) * LANE, LANE), win)

    def blk(b):
        return pl.ds(pl.multiple_of(b * BLK, BLK), BLK)

    def wrows(b):
        return pl.ds(pl.multiple_of(b * rows, rows), rows)

    def across(i):
        return [me, me + 1 - 2 * lax.rem(me, 2), me + 2 - 4 * (me // 2), 3 - me][i]

    def ahead(i):
        return across(i) if square else lax.rem(me + i, n)

    def behind(i):
        return across(i) if square else lax.rem(me + n - i, n)

    def zpeer(i):
        return lax.rem(z + i, nz) * 2 + core

    def zbehind(i):
        return lax.rem(z + nz - i, nz)

    def copy(src, dst, ss, rs, dev):
        return pltpu.make_async_remote_copy(
            src_ref=src, dst_ref=dst, send_sem=ss, recv_sem=rs, device_id=dev, device_id_type=MESH
        )

    barrier = pltpu.get_barrier_semaphore()
    for i in range(1, n):
        pl.semaphore_signal(barrier, inc=1, device_id=(d, ahead(i)), device_id_type=MESH)
    for i in range(1, nz):
        pl.semaphore_signal(barrier, inc=1, device_id=(zpeer(i), me), device_id_type=MESH)
    pl.semaphore_signal(barrier, inc=1, device_id=(partner, me), device_id_type=MESH)
    pl.semaphore_wait(barrier, n + nz - 1)

    def kv_copies(i, block, dev):
        return [
            copy(k, kbuf.at[blk(block), :], kv_s.at[0, i], kv_r.at[0, i], (d, dev)),
            copy(v, vbuf.at[blk(block), :], kv_s.at[1, i], kv_r.at[1, i], (d, dev)),
        ]

    def kv_part(half, block, slot, to, own):
        held = (vbuf, kbuf)[half].at[block * BLK : (block + 1) * BLK, :]
        src = (v, k)[half] if own else held
        return copy(src, held, kv_s.at[half, slot], kv_r.at[half, slot], (d, to))

    kv_first = {
        0: [(0, 0, 1, 1), (1, 0, 2, 2), (0, 0, 2, 2), (1, 0, 1, 1)],
        1: [(0, 1, 2, 3), (1, 1, 2, 3)],
        2: [(1, 2, 1, 3), (0, 2, 1, 3)],
        3: [],
    }
    kv_then = {
        0: [],
        1: [(0, 0, 1, (3, 3)), (1, 0, 1, None)],
        2: [(1, 0, 2, (3, 3)), (0, 0, 2, None), (0, 1, 1, None), (1, 1, 1, None)],
        3: [
            (0, 1, 2, (1, 2)), (1, 1, 2, (1, 2)), (0, 2, 1, None), (1, 2, 1, None),
            (0, 0, 3, None), (1, 0, 3, None),
        ],
    }
    if square:
        for r in range(n):
            @pl.when(me == r)
            def _(r=r):
                for half, block, slot, to in kv_first[r]:
                    kv_part(half, block, slot, to, True).start()
    else:
        for i in range(1, n):
            @pl.when(ahead(i) > me)
            def _(i=i):
                for c in kv_copies(i, me, ahead(i)):
                    c.start()

    def w_copy(i):
        return copy(w.at[:, window(me)], wc.at[wrows(d), :], w_s.at[i], w_r.at[i], (zpeer(i), me))

    def w_arrived(i):
        there = wc.at[wrows(zbehind(i) * 2 + core), :]
        return copy(there, there, w_s.at[i], w_r.at[i], (zpeer(i), me))

    def w_relay(i):
        there = wc.at[wrows(zbehind(i) * 2 + core), :]
        src = w.at[:, window(me)] if i == 0 else there
        return copy(src, there, wp_s.at[i], wp_r.at[i], (partner, me))

    def w_relayed(i):
        there = wc.at[wrows(zbehind(i) * 2 + 1 - core), :]
        return copy(there, there, wp_s.at[i], wp_r.at[i], (partner, me))

    for i in range(1, nz):
        w_copy(i).start()
    w_relay(0).start()
    wc[wrows(d), :] = w[:, window(me)]
    kbuf[blk(me), :] = k[...]
    vbuf[blk(me), :] = v[...]
    goc[blk(me), :] = go[:, window(me)]
    for u in range(1, n):
        @pl.when(u > me)
        def _(u=u):
            kbuf[u * BLK : (u + 1) * BLK, :] = jnp.zeros((BLK, kbuf.shape[1]), BF16)
            vbuf[u * BLK : (u + 1) * BLK, :] = jnp.zeros((BLK, vbuf.shape[1]), BF16)

    if square:
        for r in range(n):
            @pl.when(me == r)
            def _(r=r):
                for half, block, slot, relay in kv_then[r]:
                    kv_part(half, block, slot, r - 1 if r else 1, False).wait_recv()
                    if relay:
                        kv_part(half, block, relay[0], relay[1], False).start()
                for half, block, slot, to in kv_first[r]:
                    kv_part(half, block, slot, to, True).wait_send()
                for half, block, slot, relay in kv_then[r]:
                    if relay:
                        kv_part(half, block, relay[0], relay[1], False).wait_send()
    else:
        for i in range(1, n):
            @pl.when(behind(i) < me)
            def _(i=i):
                for c in kv_copies(i, behind(i), ahead(i)):
                    c.wait_recv()

    def go_copy(i, block):
        return copy(
            go.at[:, window(ahead(i))], goc.at[blk(block), :], go_s.at[i], go_r.at[i], (d, ahead(i))
        )

    for i in range(1, n):
        go_copy(i, me).start()

    qpos = lax.rem(lax.broadcasted_iota(jnp.int32, (2 * BLK, keys), 0), BLK)
    kpos = lax.broadcasted_iota(jnp.int32, (2 * BLK, keys), 1)
    allowed = (kpos <= qpos + me * BLK) & (kpos >= me * BLK)
    for s in range(TOPK):
        first = bl[0, s] * BLK
        allowed = allowed | ((kpos >= first) & (kpos < first + BLK) & (kpos >= 0))

    def pair(x, j):
        return jnp.concatenate(
            [x[:, 2 * j * HD : (2 * j + 1) * HD], x[:, (2 * j + 1) * HD : (2 * j + 2) * HD]], axis=0
        )

    def h_copy(j, i, block):
        ref = hall.at[blk(block), pl.ds(j * 2 * HD, 2 * HD)]
        return copy(ref, ref, h_s.at[j, i], h_r.at[j, i], (d, ahead(i)))

    def relayed(part):
        def send(half, hop, block):
            to = hop if hop < 3 else 2 - half
            return part(half, hop, to, block)

        return send

    def relay_on(send):
        for half in range(2):
            send(half, half + 1, across(half + 1)).wait_recv()
            send(half, 3, across(half + 1)).start()

    def relay_end(send):
        for half in range(2):
            send(half, 2 - half, across(2 - half)).wait_recv()
            send(half, 3, across(3)).wait_recv()

    def relay_drain(send):
        for half in range(2):
            for hop in (1, 2):
                send(half, hop, me).wait_send()
            send(half, 3, across(half + 1)).wait_send()

    def h_part(half, slot, to, block):
        ref = hall.at[blk(block), pl.ds(half * 2 * HD, 2 * HD)]
        return copy(ref, ref, h_s.at[half, slot], h_r.at[half, slot], (d, across(to)))

    def wo_part(half, slot, to, block):
        ref = wog.at[block, pl.ds(half * (rows // 2), rows // 2), :]
        return copy(ref, ref, wo_s.at[half, slot], wo_r.at[half, slot], (d, across(to)))

    h_send, wo_send = relayed(h_part), relayed(wo_part)

    for j in range(HK):
        logits = dot(pair(q, j), kbuf[:, j * HD : (j + 1) * HD], NT) * SCALE
        logits = jnp.where(allowed, logits, NEGATIVE)
        e = jnp.exp(logits - jnp.max(logits, axis=-1, keepdims=True))
        p = e / jnp.sum(e, axis=-1, keepdims=True)
        probs[j] = p
        out = dot(p.astype(BF16), vbuf[:, j * HD : (j + 1) * HD], NN).astype(BF16)
        hall[blk(me), 2 * j * HD : (2 * j + 1) * HD] = out[:BLK]
        hall[blk(me), (2 * j + 1) * HD : (2 * j + 2) * HD] = out[BLK:]
        if square:
            h_send(j, j + 1, me).start()
        else:
            for i in range(1, n):
                h_copy(j, i, me).start()
    if square:
        h_send(0, 2, me).start()
        h_send(1, 1, me).start()
        relay_on(h_send)

    for i in range(1, nz):
        w_arrived(i).wait_recv()
        w_relay(i).start()
    for i in range(nz):
        w_relayed(i).wait_recv()

    col = lax.broadcasted_iota(jnp.int32, (1, win), 1) // LANE + start_of(me)
    live = (col >= tiles * me // n) & (col < tiles * (me + 1) // n)
    gain_win = gain[window(me)].reshape(1, win)
    lane = lax.broadcasted_iota(jnp.int32, (BLK, LANE), 1)
    for i in range(n):
        b = behind(i)
        if i:
            if not square:
                for j in range(HK):
                    h_copy(j, i, b).wait_recv()
            elif i < 3:
                h_send(2 - i, i, b).wait_recv()
            else:
                h_send(0, 3, b).wait_recv()
                h_send(1, 3, b).wait_recv()
            go_copy(i, b).wait_recv()
        part = jnp.where(live, dot(hall[blk(b), :], wc[...], NN), 0.0)
        mixed[blk(b), :] = part
        scaled = goc[blk(b), :].astype(F32) * gain_win
        energy = jnp.sum(part * part, axis=-1, keepdims=True)
        cross = jnp.sum(scaled * part, axis=-1, keepdims=True)
        both = jnp.where(lane == 0, energy, jnp.where(lane == 1, cross, 0.0))
        stat[me, b] = jnp.transpose(both)[:8]

    def st_copy(i, slot):
        return copy(stat.at[slot], stat.at[slot], st_s.at[i], st_r.at[i], (d, ahead(i)))

    for i in range(1, n):
        st_copy(i, me).start()
    for i in range(1, n):
        st_copy(i, behind(i)).wait_recv()

    def gh_copy(i):
        return copy(ghs.at[i], ghr.at[i], gh_s.at[i], gh_r.at[i], (d, ahead(i)))

    gain_part = jnp.zeros((1, win), F32)
    for step in range(n):
        i = (step + 1) % n
        b = ahead(i)
        total = stat[0, b]
        for c in range(1, n):
            total = total + stat[c, b]
        turned = jnp.transpose(jnp.concatenate([total] * (LANE // 8), axis=0))
        inv = lax.rsqrt(turned[:, 0:1] / width + EPSILON)
        cross = turned[:, 1:2] / width
        part = mixed[blk(b), :]
        upstream = goc[blk(b), :].astype(F32)
        grad = inv * (upstream * gain_win - part * (inv * inv * cross))
        grad = jnp.where(live, grad, 0.0).astype(BF16)
        gm[blk(b), :] = grad
        back = dot(grad, wc[...], NT)
        if i:
            ghs[i] = back.astype(BF16)
            gh_copy(i).start()
        else:
            gho[...] = back
        gain_part = gain_part + jnp.sum(upstream * part * inv, axis=0, keepdims=True)
    gp[...] = jnp.broadcast_to(gain_part, (8, win))

    def gp_copy():
        return copy(gp, gpr, gn_s.at[0], gn_r.at[0], (partner, me))

    gp_copy().start()

    for j in range(HQ):
        both = dot(hall[:, j * HD : (j + 1) * HD], gm[...], TN)
        gwf[j * HD : (j + 1) * HD, :] = both
        gws[j * HD : (j + 1) * HD, :] = both.astype(BF16)

    def gw_copy(zz):
        return copy(
            gws.at[wrows(zz * 2 + 1 - core), :], gwr.at[zz], gw_s.at[zz], gw_r.at[zz], (partner, me)
        )

    def z_copy(i):
        return copy(zs.at[i], zr.at[i], z_s.at[i], z_r.at[i], (zpeer(i), me))

    def gz_copy(i, slot):
        return copy(gz.at[slot], gz.at[slot], gn_s.at[i], gn_r.at[i], (zpeer(i), me))

    for zz in range(nz):
        gw_copy(zz).start()
    gp_copy().wait_recv()
    gz[z] = gp[...] + gpr[...]
    for zz in range(nz):
        gw_copy(zz).wait_recv()
    for i in range(1, nz):
        zz = lax.rem(z + i, nz)
        zs[i] = (gwf[wrows(zz * 2 + core), :] + gwr[zz].astype(F32)).astype(BF16)
        z_copy(i).start()
        gz_copy(i, z).start()

    back = gho[...]
    for i in range(1, n):
        gh_copy(i).wait_recv()
        back = back + ghr[i].astype(F32)
    back = back.astype(BF16)
    held = hall[blk(me), :]
    for j in range(HK):
        gj = pair(back, j)
        oj = pair(held, j)
        delta = jnp.sum(gj.astype(F32) * oj.astype(F32), axis=-1, keepdims=True)
        span = slice(j * HD, (j + 1) * HD)
        gprob = dot(gj, vbuf[:, span], NT)
        p = probs[j]
        ds = (p * (gprob - delta) * SCALE).astype(BF16)
        dv = dot(p.astype(BF16), gj, TN)
        dk = dot(ds, pair(q, j), TN)
        dvf[:, span] = dv
        dkf[:, span] = dk
        dvs[:, span] = dv.astype(BF16)
        dks[:, span] = dk.astype(BF16)
        dq = dot(ds, kbuf[:, span], NN).astype(BF16)
        dq_o[:, 2 * j * HD : (2 * j + 1) * HD] = dq[:BLK]
        dq_o[:, (2 * j + 1) * HD : (2 * j + 2) * HD] = dq[BLK:]

    def d_copies(i):
        dev = (d, behind(i))
        return [
            copy(dks.at[blk(behind(i)), :], dkr.at[i], d_s.at[0, i], d_r.at[0, i], dev),
            copy(dvs.at[blk(behind(i)), :], dvr.at[i], d_s.at[1, i], d_r.at[1, i], dev),
        ]

    for i in range(1, n):
        @pl.when(behind(i) < me)
        def _(i=i):
            for c in d_copies(i):
                c.start()

    total = gwf[wrows(d), :] + gwr[z].astype(F32)
    for i in range(1, nz):
        z_copy(i).wait_recv()
        total = total + zr[i].astype(F32)
        gz_copy(i, zbehind(i)).wait_recv()
    wog[me] = total.astype(BF16)
    small = gz[0]
    for zz in range(1, nz):
        small = small + gz[zz]
    gg[me] = small

    def wo_copy(i, slot):
        return copy(wog.at[slot], wog.at[slot], wo_s.at[0, i], wo_r.at[0, i], (d, ahead(i)))

    def gg_copy(i, slot):
        return copy(gg.at[slot], gg.at[slot], gg_s.at[i], gg_r.at[i], (d, ahead(i)))

    if square:
        for half, hop in ((0, 1), (1, 2), (0, 2), (1, 1)):
            wo_send(half, hop, me).start()
    for i in range(1, n):
        if not square:
            wo_copy(i, me).start()
        gg_copy(i, me).start()
    if square:
        relay_on(wo_send)

    dkf[blk(0), :] = dkf[blk(me), :]
    dvf[blk(0), :] = dvf[blk(me), :]
    for i in range(1, n):
        @pl.when(ahead(i) > me)
        def _(i=i):
            for c in d_copies(i):
                c.wait_recv()
            dkf[blk(0), :] += dkr[i].astype(F32)
            dvf[blk(0), :] += dvr[i].astype(F32)

    dk_o[...] = dkf[blk(0), :].astype(BF16)
    dv_o[...] = dvf[blk(0), :].astype(BF16)

    if square:
        relay_end(wo_send)
    for i in range(1, n):
        if not square:
            wo_copy(i, behind(i)).wait_recv()
        gg_copy(i, behind(i)).wait_recv()
    for c in range(n):
        lo, hi = tiles * c // n, tiles * (c + 1) // n
        at = (lo - start_of(c)) * LANE
        span = slice(lo * LANE, hi * LANE)
        wo_o[:, span] = wog[c, :, at : at + (hi - lo) * LANE]
        gain_o[span] = gg[c, 0, at : at + (hi - lo) * LANE] / seqs

    if square:
        relay_drain(h_send)
        relay_drain(wo_send)
    for i in range(1, n):
        @pl.when(behind(i) < me)
        def _(i=i):
            for c in d_copies(i):
                c.wait_send()

        if not square:
            @pl.when(ahead(i) > me)
            def _(i=i):
                for c in kv_copies(i, me, ahead(i)):
                    c.wait_send()

            for j in range(HK):
                h_copy(j, i, me).wait_send()
            wo_copy(i, me).wait_send()
        go_copy(i, me).wait_send()
        st_copy(i, me).wait_send()
        gh_copy(i).wait_send()
        gg_copy(i, me).wait_send()
    for i in range(1, nz):
        w_copy(i).wait_send()
        z_copy(i).wait_send()
        gz_copy(i, z).wait_send()
    for i in range(nz):
        w_relay(i).wait_send()
        gw_copy(i).wait_send()
    gp_copy().wait_send()


def per_device(n, ndp, query, key, value, out_weight, post_gain, grad_out, block_lists):
    width = out_weight.shape[1]
    rows = out_weight.shape[0]
    tiles = width // LANE
    win = -(-tiles // n) * LANE
    keys = n * BLK
    nz = ndp // 2
    qw, kw = HQ * HD, HK * HD
    vm = pl.BlockSpec(memory_space=pltpu.VMEM)
    dma = pltpu.SemaphoreType.DMA
    dq, dk, dv, wo, gain = pl.pallas_call(
        functools.partial(kernel, n, ndp),
        out_shape=(
            jax.ShapeDtypeStruct((BLK, qw), BF16),
            jax.ShapeDtypeStruct((BLK, kw), BF16),
            jax.ShapeDtypeStruct((BLK, kw), BF16),
            jax.ShapeDtypeStruct((rows, width), BF16),
            jax.ShapeDtypeStruct((width,), F32),
        ),
        in_specs=[vm] * 6 + [pl.BlockSpec(memory_space=pltpu.SMEM)],
        out_specs=[vm] * 5,
        scratch_shapes=[
            pltpu.VMEM((keys, kw), BF16),
            pltpu.VMEM((keys, kw), BF16),
            pltpu.VMEM((qw, win), BF16),
            pltpu.VMEM((keys, win), BF16),
            pltpu.VMEM((keys, qw), BF16),
            pltpu.VMEM((HK, 2 * BLK, keys), F32),
            pltpu.VMEM((keys, win), F32),
            pltpu.VMEM((keys, win), BF16),
            pltpu.VMEM((n, n, 8, LANE), F32),
            pltpu.VMEM((n, BLK, qw), BF16),
            pltpu.VMEM((n, BLK, qw), BF16),
            pltpu.VMEM((BLK, qw), F32),
            pltpu.VMEM((qw, win), F32),
            pltpu.VMEM((qw, win), BF16),
            pltpu.VMEM((nz, rows, win), BF16),
            pltpu.VMEM((nz, rows, win), BF16),
            pltpu.VMEM((nz, rows, win), BF16),
            pltpu.VMEM((keys, kw), F32),
            pltpu.VMEM((keys, kw), F32),
            pltpu.VMEM((keys, kw), BF16),
            pltpu.VMEM((keys, kw), BF16),
            pltpu.VMEM((n, BLK, kw), BF16),
            pltpu.VMEM((n, BLK, kw), BF16),
            pltpu.VMEM((n, rows, win), BF16),
            pltpu.VMEM((8, win), F32),
            pltpu.VMEM((8, win), F32),
            pltpu.VMEM((nz, 8, win), F32),
            pltpu.VMEM((n, 8, win), F32),
            dma((2, n)), dma((2, n)), dma((nz,)), dma((nz,)), dma((nz,)), dma((nz,)),
            dma((n,)), dma((n,)), dma((HK, n)), dma((HK, n)), dma((n,)), dma((n,)),
            dma((n,)), dma((n,)), dma((nz,)), dma((nz,)), dma((nz,)), dma((nz,)),
            dma((2, n)), dma((2, n)), dma((2, n)), dma((2, n)), dma((nz,)), dma((nz,)), dma((n,)), dma((n,)),
        ],
        compiler_params=pltpu.CompilerParams(
            collective_id=0, has_side_effects=True, vmem_limit_bytes=56 * 2**20
        ),
        cost_estimate=pl.CostEstimate(flops=4 * 10**9, bytes_accessed=6 * 10**6, transcendentals=262144),
    )(
        query[0], key[0], value[0], out_weight, post_gain, grad_out[0], block_lists[0],
    )
    return (dq[None], dk[None], dv[None], wo.astype(F32) / ndp, gain)


def solution(mesh):
    n, ndp = mesh.shape["ctx"], mesh.shape["dp"]
    seq = P("dp", "ctx", None)
    return jax.shard_map(
        functools.partial(per_device, n, ndp),
        mesh=mesh,
        in_specs=(seq, seq, seq, P("dp", None), P(), seq, seq),
        out_specs=(seq, seq, seq, P("dp", None), P()),
        check_vma=False,
    )
```

```python
import functools
import jax
import jax.numpy as jnp
from jax import lax
from jax.experimental import pallas as pl
from jax.experimental.pallas import tpu as pltpu
from jax.sharding import PartitionSpec as P

HD = 256
HQ = 4
HK = 2
BLK = 128
TOPK = 3
LANE = 128
SCALE = 0.0625
NEGATIVE = -1e30
EPSILON = 1e-06
MESH = pl.DeviceIdType.MESH
F32 = jnp.float32
BF16 = jnp.bfloat16


def dot(a, b, dims):
    return lax.dot_general(a, b, (dims, ((), ())), preferred_element_type=F32)


NN = ((1,), (0,))
NT = ((1,), (1,))
TN = ((0,), (0,))


def kernel(
    n, ndp, q, k, v, w, gain, go, bl,
    dq_o, dk_o, dv_o, wo_o, gain_o,
    kbuf, vbuf, wc, goc, hall, probs, mixed, gm, stat, ghs, ghr, gho, gwf, gws, gwr, zs, zr,
    dkf, dvf, dks, dvs, dkr, dvr, wog, gp, gpr, gz, gg,
    kv_s, kv_r, w_s, w_r, wp_s, wp_r, go_s, go_r, h_s, h_r, st_s, st_r, gh_s, gh_r,
    gw_s, gw_r, z_s, z_r, d_s, d_r, wo_s, wo_r, gn_s, gn_r, gg_s, gg_r,
):
    d = lax.axis_index("dp")
    me = lax.axis_index("ctx")
    core = lax.rem(d, 2)
    z = d // 2
    nz = ndp // 2
    partner = d + 1 - 2 * core
    width = w.shape[1]
    square = n == 4
    tiles = width // LANE
    wt = -(-tiles // n)
    win = wt * LANE
    rows = w.shape[0]
    keys = n * BLK
    seqs = float(ndp)

    def start_of(c):
        if isinstance(c, int):
            return min(tiles * c // n, tiles - wt)
        return jnp.minimum(tiles * c // n, tiles - wt)

    def window(c):
        return pl.ds(pl.multiple_of(start_of(c) * LANE, LANE), win)

    def blk(b):
        return pl.ds(pl.multiple_of(b * BLK, BLK), BLK)

    def wrows(b):
        return pl.ds(pl.multiple_of(b * rows, rows), rows)

    def across(i):
        return [me, me + 1 - 2 * lax.rem(me, 2), me + 2 - 4 * (me // 2), 3 - me][i]

    def ahead(i):
        return across(i) if square else lax.rem(me + i, n)

    def behind(i):
        return across(i) if square else lax.rem(me + n - i, n)

    def zpeer(i):
        return lax.rem(z + i, nz) * 2 + core

    def zbehind(i):
        return lax.rem(z + nz - i, nz)

    def copy(src, dst, ss, rs, dev):
        return pltpu.make_async_remote_copy(
            src_ref=src, dst_ref=dst, send_sem=ss, recv_sem=rs, device_id=dev, device_id_type=MESH
        )

    barrier = pltpu.get_barrier_semaphore()
    for i in range(1, n):
        pl.semaphore_signal(barrier, inc=1, device_id=(d, ahead(i)), device_id_type=MESH)
    for i in range(1, nz):
        pl.semaphore_signal(barrier, inc=1, device_id=(zpeer(i), me), device_id_type=MESH)
    pl.semaphore_signal(barrier, inc=1, device_id=(partner, me), device_id_type=MESH)
    pl.semaphore_wait(barrier, n + nz - 1)

    def kv_copies(i, block, dev):
        return [
            copy(k, kbuf.at[blk(block), :], kv_s.at[0, i], kv_r.at[0, i], (d, dev)),
            copy(v, vbuf.at[blk(block), :], kv_s.at[1, i], kv_r.at[1, i], (d, dev)),
        ]

    def kv_part(half, block, slot, to, own):
        held = (vbuf, kbuf)[half].at[block * BLK : (block + 1) * BLK, :]
        src = (v, k)[half] if own else held
        return copy(src, held, kv_s.at[half, slot], kv_r.at[half, slot], (d, to))

    kv_first = {
        0: [(0, 0, 1, 1), (1, 0, 2, 2), (0, 0, 2, 2), (1, 0, 1, 1)],
        1: [(0, 1, 2, 3), (1, 1, 2, 3)],
        2: [(1, 2, 1, 3), (0, 2, 1, 3)],
        3: [],
    }
    kv_then = {
        0: [],
        1: [(0, 0, 1, (3, 3)), (1, 0, 1, None)],
        2: [(1, 0, 2, (3, 3)), (0, 0, 2, None), (0, 1, 1, None), (1, 1, 1, None)],
        3: [
            (0, 1, 2, (1, 2)), (1, 1, 2, (1, 2)), (0, 2, 1, None), (1, 2, 1, None),
            (0, 0, 3, None), (1, 0, 3, None),
        ],
    }
    if square:
        for r in range(n):
            @pl.when(me == r)
            def _(r=r):
                for half, block, slot, to in kv_first[r]:
                    kv_part(half, block, slot, to, True).start()
    else:
        for i in range(1, n):
            @pl.when(ahead(i) > me)
            def _(i=i):
                for c in kv_copies(i, me, ahead(i)):
                    c.start()

    def w_copy(i):
        return copy(w.at[:, window(me)], wc.at[wrows(d), :], w_s.at[i], w_r.at[i], (zpeer(i), me))

    def w_arrived(i):
        there = wc.at[wrows(zbehind(i) * 2 + core), :]
        return copy(there, there, w_s.at[i], w_r.at[i], (zpeer(i), me))

    def w_relay(i):
        there = wc.at[wrows(zbehind(i) * 2 + core), :]
        src = w.at[:, window(me)] if i == 0 else there
        return copy(src, there, wp_s.at[i], wp_r.at[i], (partner, me))

    def w_relayed(i):
        there = wc.at[wrows(zbehind(i) * 2 + 1 - core), :]
        return copy(there, there, wp_s.at[i], wp_r.at[i], (partner, me))

    for i in range(1, nz):
        w_copy(i).start()
    w_relay(0).start()
    wc[wrows(d), :] = w[:, window(me)]
    kbuf[blk(me), :] = k[...]
    vbuf[blk(me), :] = v[...]
    goc[blk(me), :] = go[:, window(me)]
    for u in range(1, n):
        @pl.when(u > me)
        def _(u=u):
            kbuf[u * BLK : (u + 1) * BLK, :] = jnp.zeros((BLK, kbuf.shape[1]), BF16)
            vbuf[u * BLK : (u + 1) * BLK, :] = jnp.zeros((BLK, vbuf.shape[1]), BF16)

    if square:
        for r in range(n):
            @pl.when(me == r)
            def _(r=r):
                for half, block, slot, relay in kv_then[r]:
                    kv_part(half, block, slot, r - 1 if r else 1, False).wait_recv()
                    if relay:
                        kv_part(half, block, relay[0], relay[1], False).start()
                for half, block, slot, to in kv_first[r]:
                    kv_part(half, block, slot, to, True).wait_send()
                for half, block, slot, relay in kv_then[r]:
                    if relay:
                        kv_part(half, block, relay[0], relay[1], False).wait_send()
    else:
        for i in range(1, n):
            @pl.when(behind(i) < me)
            def _(i=i):
                for c in kv_copies(i, behind(i), ahead(i)):
                    c.wait_recv()

    def go_copy(i, block):
        return copy(
            go.at[:, window(ahead(i))], goc.at[blk(block), :], go_s.at[i], go_r.at[i], (d, ahead(i))
        )


    qpos = lax.rem(lax.broadcasted_iota(jnp.int32, (2 * BLK, keys), 0), BLK)
    kpos = lax.broadcasted_iota(jnp.int32, (2 * BLK, keys), 1)
    allowed = (kpos <= qpos + me * BLK) & (kpos >= me * BLK)
    for s in range(TOPK):
        first = bl[0, s] * BLK
        allowed = allowed | ((kpos >= first) & (kpos < first + BLK) & (kpos >= 0))

    def pair(x, j):
        return jnp.concatenate(
            [x[:, 2 * j * HD : (2 * j + 1) * HD], x[:, (2 * j + 1) * HD : (2 * j + 2) * HD]], axis=0
        )

    def h_copy(j, i, block):
        ref = hall.at[blk(block), pl.ds(j * 2 * HD, 2 * HD)]
        return copy(ref, ref, h_s.at[j, i], h_r.at[j, i], (d, ahead(i)))

    def relayed(part):
        def send(half, hop, block):
            to = hop if hop < 3 else 2 - half
            return part(half, hop, to, block)

        return send

    def relay_on(send):
        for half in range(2):
            send(half, half + 1, across(half + 1)).wait_recv()
            send(half, 3, across(half + 1)).start()

    def relay_end(send):
        for half in range(2):
            send(half, 2 - half, across(2 - half)).wait_recv()
            send(half, 3, across(3)).wait_recv()

    def relay_drain(send):
        for half in range(2):
            for hop in (1, 2):
                send(half, hop, me).wait_send()
            send(half, 3, across(half + 1)).wait_send()

    def h_part(half, slot, to, block):
        ref = hall.at[blk(block), pl.ds(half * 2 * HD, 2 * HD)]
        return copy(ref, ref, h_s.at[half, slot], h_r.at[half, slot], (d, across(to)))

    def wo_part(half, slot, to, block):
        ref = wog.at[block, pl.ds(half * (rows // 2), rows // 2), :]
        return copy(ref, ref, wo_s.at[half, slot], wo_r.at[half, slot], (d, across(to)))

    h_send, wo_send = relayed(h_part), relayed(wo_part)

    for j in range(HK):
        logits = dot(pair(q, j), kbuf[:, j * HD : (j + 1) * HD], NT) * SCALE
        logits = jnp.where(allowed, logits, NEGATIVE)
        e = jnp.exp(logits - jnp.max(logits, axis=-1, keepdims=True))
        p = e / jnp.sum(e, axis=-1, keepdims=True)
        probs[j] = p
        out = dot(p.astype(BF16), vbuf[:, j * HD : (j + 1) * HD], NN).astype(BF16)
        hall[blk(me), 2 * j * HD : (2 * j + 1) * HD] = out[:BLK]
        hall[blk(me), (2 * j + 1) * HD : (2 * j + 2) * HD] = out[BLK:]
        if square:
            h_send(j, j + 1, me).start()
        else:
            for i in range(1, n):
                h_copy(j, i, me).start()
    if square:
        h_send(0, 2, me).start()
        h_send(1, 1, me).start()
        relay_on(h_send)
    for i in range(1, n):
        go_copy(i, me).start()

    for i in range(1, nz):
        w_arrived(i).wait_recv()
        w_relay(i).start()
    for i in range(nz):
        w_relayed(i).wait_recv()

    col = lax.broadcasted_iota(jnp.int32, (1, win), 1) // LANE + start_of(me)
    live = (col >= tiles * me // n) & (col < tiles * (me + 1) // n)
    gain_win = gain[window(me)].reshape(1, win)
    lane = lax.broadcasted_iota(jnp.int32, (BLK, LANE), 1)
    for i in range(n):
        b = behind(i)
        if i:
            if not square:
                for j in range(HK):
                    h_copy(j, i, b).wait_recv()
            elif i < 3:
                h_send(2 - i, i, b).wait_recv()
            else:
                h_send(0, 3, b).wait_recv()
                h_send(1, 3, b).wait_recv()
            go_copy(i, b).wait_recv()
        part = jnp.where(live, dot(hall[blk(b), :], wc[...], NN), 0.0)
        mixed[blk(b), :] = part
        scaled = goc[blk(b), :].astype(F32) * gain_win
        energy = jnp.sum(part * part, axis=-1, keepdims=True)
        cross = jnp.sum(scaled * part, axis=-1, keepdims=True)
        both = jnp.where(lane == 0, energy, jnp.where(lane == 1, cross, 0.0))
        stat[me, b] = jnp.transpose(both)[:8]

    def st_copy(i, slot):
        return copy(stat.at[slot], stat.at[slot], st_s.at[i], st_r.at[i], (d, ahead(i)))

    for i in range(1, n):
        st_copy(i, me).start()
    for i in range(1, n):
        st_copy(i, behind(i)).wait_recv()

    def gh_copy(i):
        return copy(ghs.at[i], ghr.at[i], gh_s.at[i], gh_r.at[i], (d, ahead(i)))

    gain_part = jnp.zeros((1, win), F32)
    for step in range(n):
        i = (step + 1) % n
        b = ahead(i)
        total = stat[0, b]
        for c in range(1, n):
            total = total + stat[c, b]
        turned = jnp.transpose(jnp.concatenate([total] * (LANE // 8), axis=0))
        inv = lax.rsqrt(turned[:, 0:1] / width + EPSILON)
        cross = turned[:, 1:2] / width
        part = mixed[blk(b), :]
        upstream = goc[blk(b), :].astype(F32)
        grad = inv * (upstream * gain_win - part * (inv * inv * cross))
        grad = jnp.where(live, grad, 0.0).astype(BF16)
        gm[blk(b), :] = grad
        back = dot(grad, wc[...], NT)
        if i:
            ghs[i] = back.astype(BF16)
            gh_copy(i).start()
        else:
            gho[...] = back
        gain_part = gain_part + jnp.sum(upstream * part * inv, axis=0, keepdims=True)
    gp[...] = jnp.broadcast_to(gain_part, (8, win))

    def gp_copy():
        return copy(gp, gpr, gn_s.at[0], gn_r.at[0], (partner, me))

    gp_copy().start()

    for j in range(HQ):
        both = dot(hall[:, j * HD : (j + 1) * HD], gm[...], TN)
        gwf[j * HD : (j + 1) * HD, :] = both
        gws[j * HD : (j + 1) * HD, :] = both.astype(BF16)

    def gw_copy(zz):
        return copy(
            gws.at[wrows(zz * 2 + 1 - core), :], gwr.at[zz], gw_s.at[zz], gw_r.at[zz], (partner, me)
        )

    def z_copy(i):
        return copy(zs.at[i], zr.at[i], z_s.at[i], z_r.at[i], (zpeer(i), me))

    def gz_copy(i, slot):
        return copy(gz.at[slot], gz.at[slot], gn_s.at[i], gn_r.at[i], (zpeer(i), me))

    for zz in range(nz):
        gw_copy(zz).start()
    gp_copy().wait_recv()
    gz[z] = gp[...] + gpr[...]
    for zz in range(nz):
        gw_copy(zz).wait_recv()
    for i in range(1, nz):
        zz = lax.rem(z + i, nz)
        zs[i] = (gwf[wrows(zz * 2 + core), :] + gwr[zz].astype(F32)).astype(BF16)
        z_copy(i).start()
        gz_copy(i, z).start()

    back = gho[...]
    for i in range(1, n):
        gh_copy(i).wait_recv()
        back = back + ghr[i].astype(F32)
    back = back.astype(BF16)
    held = hall[blk(me), :]
    for j in range(HK):
        gj = pair(back, j)
        oj = pair(held, j)
        delta = jnp.sum(gj.astype(F32) * oj.astype(F32), axis=-1, keepdims=True)
        span = slice(j * HD, (j + 1) * HD)
        gprob = dot(gj, vbuf[:, span], NT)
        p = probs[j]
        ds = (p * (gprob - delta) * SCALE).astype(BF16)
        dv = dot(p.astype(BF16), gj, TN)
        dk = dot(ds, pair(q, j), TN)
        dvf[:, span] = dv
        dkf[:, span] = dk
        dvs[:, span] = dv.astype(BF16)
        dks[:, span] = dk.astype(BF16)
        dq = dot(ds, kbuf[:, span], NN).astype(BF16)
        dq_o[:, 2 * j * HD : (2 * j + 1) * HD] = dq[:BLK]
        dq_o[:, (2 * j + 1) * HD : (2 * j + 2) * HD] = dq[BLK:]

    def d_copies(i):
        dev = (d, behind(i))
        return [
            copy(dks.at[blk(behind(i)), :], dkr.at[i], d_s.at[0, i], d_r.at[0, i], dev),
            copy(dvs.at[blk(behind(i)), :], dvr.at[i], d_s.at[1, i], d_r.at[1, i], dev),
        ]

    for i in range(1, n):
        @pl.when(behind(i) < me)
        def _(i=i):
            for c in d_copies(i):
                c.start()

    total = gwf[wrows(d), :] + gwr[z].astype(F32)
    for i in range(1, nz):
        z_copy(i).wait_recv()
        total = total + zr[i].astype(F32)
        gz_copy(i, zbehind(i)).wait_recv()
    wog[me] = total.astype(BF16)
    small = gz[0]
    for zz in range(1, nz):
        small = small + gz[zz]
    gg[me] = small

    def wo_copy(i, slot):
        return copy(wog.at[slot], wog.at[slot], wo_s.at[0, i], wo_r.at[0, i], (d, ahead(i)))

    def gg_copy(i, slot):
        return copy(gg.at[slot], gg.at[slot], gg_s.at[i], gg_r.at[i], (d, ahead(i)))

    if square:
        for half, hop in ((0, 1), (1, 2), (0, 2), (1, 1)):
            wo_send(half, hop, me).start()
    for i in range(1, n):
        if not square:
            wo_copy(i, me).start()
        gg_copy(i, me).start()
    if square:
        relay_on(wo_send)

    dkf[blk(0), :] = dkf[blk(me), :]
    dvf[blk(0), :] = dvf[blk(me), :]
    for i in range(1, n):
        @pl.when(ahead(i) > me)
        def _(i=i):
            for c in d_copies(i):
                c.wait_recv()
            dkf[blk(0), :] += dkr[i].astype(F32)
            dvf[blk(0), :] += dvr[i].astype(F32)

    dk_o[...] = dkf[blk(0), :].astype(BF16)
    dv_o[...] = dvf[blk(0), :].astype(BF16)

    if square:
        relay_end(wo_send)
    for i in range(1, n):
        if not square:
            wo_copy(i, behind(i)).wait_recv()
        gg_copy(i, behind(i)).wait_recv()
    for c in range(n):
        lo, hi = tiles * c // n, tiles * (c + 1) // n
        at = (lo - start_of(c)) * LANE
        span = slice(lo * LANE, hi * LANE)
        wo_o[:, span] = wog[c, :, at : at + (hi - lo) * LANE]
        gain_o[span] = gg[c, 0, at : at + (hi - lo) * LANE] / seqs

    if square:
        relay_drain(h_send)
        relay_drain(wo_send)
    for i in range(1, n):
        @pl.when(behind(i) < me)
        def _(i=i):
            for c in d_copies(i):
                c.wait_send()

        if not square:
            @pl.when(ahead(i) > me)
            def _(i=i):
                for c in kv_copies(i, me, ahead(i)):
                    c.wait_send()

            for j in range(HK):
                h_copy(j, i, me).wait_send()
            wo_copy(i, me).wait_send()
        go_copy(i, me).wait_send()
        st_copy(i, me).wait_send()
        gh_copy(i).wait_send()
        gg_copy(i, me).wait_send()
    for i in range(1, nz):
        w_copy(i).wait_send()
        z_copy(i).wait_send()
        gz_copy(i, z).wait_send()
    for i in range(nz):
        w_relay(i).wait_send()
        gw_copy(i).wait_send()
    gp_copy().wait_send()


def per_device(n, ndp, query, key, value, out_weight, post_gain, grad_out, block_lists):
    width = out_weight.shape[1]
    rows = out_weight.shape[0]
    tiles = width // LANE
    win = -(-tiles // n) * LANE
    keys = n * BLK
    nz = ndp // 2
    qw, kw = HQ * HD, HK * HD
    vm = pl.BlockSpec(memory_space=pltpu.VMEM)
    dma = pltpu.SemaphoreType.DMA
    dq, dk, dv, wo, gain = pl.pallas_call(
        functools.partial(kernel, n, ndp),
        out_shape=(
            jax.ShapeDtypeStruct((BLK, qw), BF16),
            jax.ShapeDtypeStruct((BLK, kw), BF16),
            jax.ShapeDtypeStruct((BLK, kw), BF16),
            jax.ShapeDtypeStruct((rows, width), BF16),
            jax.ShapeDtypeStruct((width,), F32),
        ),
        in_specs=[vm] * 6 + [pl.BlockSpec(memory_space=pltpu.SMEM)],
        out_specs=[vm] * 5,
        scratch_shapes=[
            pltpu.VMEM((keys, kw), BF16),
            pltpu.VMEM((keys, kw), BF16),
            pltpu.VMEM((qw, win), BF16),
            pltpu.VMEM((keys, win), BF16),
            pltpu.VMEM((keys, qw), BF16),
            pltpu.VMEM((HK, 2 * BLK, keys), F32),
            pltpu.VMEM((keys, win), F32),
            pltpu.VMEM((keys, win), BF16),
            pltpu.VMEM((n, n, 8, LANE), F32),
            pltpu.VMEM((n, BLK, qw), BF16),
            pltpu.VMEM((n, BLK, qw), BF16),
            pltpu.VMEM((BLK, qw), F32),
            pltpu.VMEM((qw, win), F32),
            pltpu.VMEM((qw, win), BF16),
            pltpu.VMEM((nz, rows, win), BF16),
            pltpu.VMEM((nz, rows, win), BF16),
            pltpu.VMEM((nz, rows, win), BF16),
            pltpu.VMEM((keys, kw), F32),
            pltpu.VMEM((keys, kw), F32),
            pltpu.VMEM((keys, kw), BF16),
            pltpu.VMEM((keys, kw), BF16),
            pltpu.VMEM((n, BLK, kw), BF16),
            pltpu.VMEM((n, BLK, kw), BF16),
            pltpu.VMEM((n, rows, win), BF16),
            pltpu.VMEM((8, win), F32),
            pltpu.VMEM((8, win), F32),
            pltpu.VMEM((nz, 8, win), F32),
            pltpu.VMEM((n, 8, win), F32),
            dma((2, n)), dma((2, n)), dma((nz,)), dma((nz,)), dma((nz,)), dma((nz,)),
            dma((n,)), dma((n,)), dma((HK, n)), dma((HK, n)), dma((n,)), dma((n,)),
            dma((n,)), dma((n,)), dma((nz,)), dma((nz,)), dma((nz,)), dma((nz,)),
            dma((2, n)), dma((2, n)), dma((2, n)), dma((2, n)), dma((nz,)), dma((nz,)), dma((n,)), dma((n,)),
        ],
        compiler_params=pltpu.CompilerParams(
            collective_id=0, has_side_effects=True, vmem_limit_bytes=56 * 2**20
        ),
        cost_estimate=pl.CostEstimate(flops=4 * 10**9, bytes_accessed=6 * 10**6, transcendentals=262144),
    )(
        query[0], key[0], value[0], out_weight, post_gain, grad_out[0], block_lists[0],
    )
    return (dq[None], dk[None], dv[None], wo.astype(F32) / ndp, gain)


def solution(mesh):
    n, ndp = mesh.shape["ctx"], mesh.shape["dp"]
    seq = P("dp", "ctx", None)
    return jax.shard_map(
        functools.partial(per_device, n, ndp),
        mesh=mesh,
        in_specs=(seq, seq, seq, P("dp", None), P(), seq, seq),
        out_specs=(seq, seq, seq, P("dp", None), P()),
        check_vma=False,
    )
```
